512 devices in a mesh: lon: 64 (over z, y_lo, core), lat: 8 (over x, y_hi).
Axes of the slice: x: 4, y: 8 (y_hi: 2, y_lo: 4; y = y_hi * 4 + y_lo), z: 8, core: 2. Of those that a mesh axis runs over, the one named last changes fastest.
Arguments:
- fields: bfloat16 [2, 96, 384, 512], P(None, 'lat', 'lon'), may hold values from -6 to 6
- w_fine_qkv: bfloat16 [512, 1536], P('lon'), may hold values from -0.25 to 0.25
- w_fine_out: bfloat16 [512, 512], P('lon'), may hold values from -0.25 to 0.25
- w_merge: bfloat16 [2048, 1024], P('lon'), may hold values from -0.125 to 0.125
- w_coarse_qkv: bfloat16 [1024, 3072], P('lon'), may hold values from -0.1875 to 0.1875
- w_up: bfloat16 [1024, 512], P('lon'), may hold values from -0.1875 to 0.1875
- coarse_mask: int32 [2, 48, 192], P(None, 'lat', 'lon'), may hold values 0 or 1
- cotangent: bfloat16 [2, 96, 384, 512], P(None, 'lat', 'lon'), may hold values from -6 to 6
Outputs:
- output: bfloat16 [2, 96, 384, 512], P(None, 'lat', 'lon')
- grad_fields: bfloat16 [2, 96, 384, 512], P(None, 'lat', 'lon')
The draws below stay inside these ranges and needn't reach their ends.
All inputs are finite; a program needn't handle non-finite values. No bound on the sum of `coarse_mask` on one device may be relied on, other than what follows from the above.
Results may differ from the reference program's by a relative error of at most 0.024.
Values may be sent and summed in bfloat16 or wider, within the bound.
A program may use at most 128 MiB of HBM per device.

```python
import jax
import jax.numpy as jnp
from jax import lax

C1 = 512
C2 = 1024
HD = 32
LEV = 2
WLEV = 2
WLAT = 6
WLON = 12
SHLAT = 3
SHLON = 6
NLAT = 96
NLON = 384


def place_ends(values, key, smallest, top_value):
    place = [jax.random.randint(jax.random.fold_in(key, axis), (), 0, length) for axis, length in enumerate(values.shape)]
    main_axis = values.shape.index(max(values.shape))
    beside = place[:main_axis] + [(place[main_axis] + 1) % values.shape[main_axis]] + place[main_axis + 1:]
    return values.at[tuple(place)].set(smallest).at[tuple(beside)].set(top_value)


def block_levels(own_key, dims, split, least, high):
    level = 1.0
    for axis_at, parts in split:
        heights = jax.random.uniform(jax.random.fold_in(jax.random.fold_in(own_key, 6), axis_at), (parts,), jnp.float32, least / len(split), high / len(split))
        level = level * jnp.repeat(jnp.exp(heights), dims[axis_at] // parts).reshape((-1,) + (1,) * (len(dims) - 1 - axis_at))
    return level


def normal_values(own_key, dims, scale, reach, pieces=(), kind=jnp.bfloat16):
    result = jax.random.normal(own_key, dims, jnp.float32) * scale
    if len(pieces) > 0:
        result = block_levels(own_key, dims, pieces, -0.22, 0.18) * result
    return jnp.clip(result, min=-reach, max=reach).astype(kind)


def setup_inputs(seed: int = 0) -> dict:
    keys = jax.random.split(jax.random.key(seed), 9)
    fields = normal_values(keys[0], (LEV, NLAT, NLON, C1), 1.0, 6.0, ((1, 8), (2, 64)))
    w_fine_qkv = normal_values(keys[1], (C1, 3 * C1), C1 ** -0.5, 0.25, ((0, 64),))
    w_fine_out = normal_values(keys[2], (C1, C1), C1 ** -0.5, 0.25, ((0, 64),))
    w_merge = normal_values(keys[3], (4 * C1, C2), (4 * C1) ** -0.5, 0.125, ((0, 64),))
    w_coarse_qkv = normal_values(keys[4], (C2, 3 * C2), C2 ** -0.5, 0.1875, ((0, 64),))
    w_up = normal_values(keys[5], (C2, C1), C2 ** -0.5, 0.1875, ((0, 64),))
    coarse_mask = place_ends((jax.random.randint(keys[6], (LEV, NLAT // 2, NLON // 2), 0, 4) < 3).astype(jnp.int32), jax.random.fold_in(keys[6], 1), 0, 1)
    cotangent = normal_values(keys[7], (LEV, NLAT, NLON, C1), 1.0, 6.0, ((1, 8), (2, 64)))
    return {"fields": fields, "w_fine_qkv": w_fine_qkv, "w_fine_out": w_fine_out, "w_merge": w_merge, "w_coarse_qkv": w_coarse_qkv, "w_up": w_up, "coarse_mask": coarse_mask, "cotangent": cotangent}


NORM_EPS = 1e-05
FAR_SCORE = -1000000000.0
MASK_PENALTY = 4.0

def norm_rows(values):
    wide = values.astype(jnp.float32)
    centre = lax.optimization_barrier(jnp.mean(wide, axis=-1, keepdims=True))
    spread = lax.optimization_barrier(jnp.mean(jnp.square(wide - centre), axis=-1, keepdims=True))
    return ((wide - centre) * lax.rsqrt(spread + NORM_EPS)).astype(jnp.bfloat16)

def project(values, weight):
    flat_rows = values.reshape(-1, values.shape[-1])
    product = jnp.dot(flat_rows, weight, preferred_element_type=jnp.float32)
    return product.astype(jnp.bfloat16).reshape(values.shape[:-1] + (weight.shape[1],))

def add_round(first, second):
    return (first.astype(jnp.float32) + second.astype(jnp.float32)).astype(jnp.bfloat16)

def attend(query, key_rows, value_rows, bias):
    score_scale = query.shape[-1] ** (-0.5)
    scores = jnp.einsum('bqhd,bkhd->bhqk', query.astype(jnp.float32), key_rows.astype(jnp.float32)) * score_scale
    scores = scores + bias[:, None]
    row_peak = lax.optimization_barrier(jnp.max(scores, axis=-1, keepdims=True))
    expo = jnp.exp(scores - row_peak)
    softmax_w = (expo / lax.optimization_barrier(jnp.sum(expo, axis=-1, keepdims=True))).astype(jnp.bfloat16)
    mixed = jnp.einsum('bhqk,bkhd->bqhd', softmax_w.astype(jnp.float32), value_rows.astype(jnp.float32))
    return mixed.astype(jnp.bfloat16)

def to_windows(values, win_levels, win_rows, win_cols):
    levels, lat_rows, lon_cols = values.shape[:3]
    trailing = values.shape[3:]
    values = values.reshape((levels // win_levels, win_levels, lat_rows // win_rows, win_rows, lon_cols // win_cols, win_cols) + trailing)
    perm_axes = (0, 2, 4, 1, 3, 5) + tuple(range(6, 6 + len(trailing)))
    values = jnp.transpose(values, perm_axes)
    count = levels // win_levels * (lat_rows // win_rows) * (lon_cols // win_cols)
    return values.reshape((count, win_levels * win_rows * win_cols) + trailing)

def from_windows(windows, levels, lat_rows, lon_cols, win_levels, win_rows, win_cols):
    trailing = windows.shape[2:]
    windows = windows.reshape((levels // win_levels, lat_rows // win_rows, lon_cols // win_cols, win_levels, win_rows, win_cols) + trailing)
    perm_axes = (0, 3, 1, 4, 2, 5) + tuple(range(6, 6 + len(trailing)))
    return jnp.transpose(windows, perm_axes).reshape((levels, lat_rows, lon_cols) + trailing)

def fine_block(rolled, w_qkv, w_out, seam_rows):
    levels, lat_rows, lon_cols, channels = rolled.shape
    heads = channels // HD
    qkv = project(norm_rows(rolled), w_qkv).reshape(levels, lat_rows, lon_cols, 3, heads, HD)
    windows = to_windows(qkv, WLEV, WLAT, WLON)
    region = jnp.broadcast_to(seam_rows[None, :, None], (levels, lat_rows, lon_cols)).astype(jnp.float32)
    region_win = to_windows(region, WLEV, WLAT, WLON)
    bias = jnp.where(region_win[:, :, None] == region_win[:, None, :], jnp.float32(0.0), jnp.float32(FAR_SCORE))
    mixed = attend(windows[:, :, 0], windows[:, :, 1], windows[:, :, 2], bias)
    mixed = from_windows(mixed, levels, lat_rows, lon_cols, WLEV, WLAT, WLON).reshape(levels, lat_rows, lon_cols, channels)
    return project(mixed, w_out)

def merge_block(fine, w_merge):
    levels, lat_rows, lon_cols, channels = fine.shape
    grouped = fine.reshape(levels, lat_rows // 2, 2, lon_cols // 2, 2, channels)
    grouped = jnp.transpose(grouped, (0, 1, 3, 2, 4, 5)).reshape(levels, lat_rows // 2, lon_cols // 2, 4 * channels)
    return project(norm_rows(grouped), w_merge)

def tail_block(fine, deeper, w_up):
    upward = project(deeper, w_up)
    spread_up = jnp.repeat(jnp.repeat(upward, 2, axis=1), 2, axis=2)
    return add_round(fine, spread_up)

def reference(fields, w_fine_qkv, w_fine_out, w_merge, w_coarse_qkv, w_up, coarse_mask, cotangent):
    seam_rows = jnp.arange(NLAT) >= NLAT - SHLAT
    mask_float = coarse_mask.astype(jnp.float32)

    def forward(inputs):
        rolled = jnp.roll(inputs, (-SHLAT, -SHLON), axis=(1, 2))
        mixed = jax.checkpoint(fine_block)(rolled, w_fine_qkv, w_fine_out, seam_rows)
        skip = add_round(inputs, jnp.roll(mixed, (SHLAT, SHLON), axis=(1, 2)))
        coarse = merge_block(skip, w_merge)
        levels, lat_rows, lon_cols, channels = coarse.shape
        normed = norm_rows(coarse)
        qkv = project(normed, w_coarse_qkv).reshape(levels, lat_rows, lon_cols, 3, channels // HD, HD)
        windows = to_windows(qkv, WLEV, WLAT, WLON)
        mask_win = to_windows(mask_float, WLEV, WLAT, WLON)
        bias = (-MASK_PENALTY * (1.0 - mask_win))[:, None, :]
        attended = attend(windows[:, :, 0], windows[:, :, 1], windows[:, :, 2], bias)
        attended = from_windows(attended, levels, lat_rows, lon_cols, WLEV, WLAT, WLON).reshape(levels, lat_rows, lon_cols, channels)
        deeper = add_round(coarse, attended)
        return tail_block(skip, deeper, w_up)
    output, pullback = jax.vjp(forward, fields)
    grad_fields, = pullback(cotangent)
    return (output, grad_fields)
```

```python
import jax
import jax.numpy as jnp
from jax import lax
from jax.experimental import pallas as pl
from jax.experimental.pallas import tpu as pltpu
from jax.sharding import PartitionSpec as P

HD = 32
WLEV = 2
WLAT = 6
SHLAT = 3
SHLON = 6


NORM_EPS = 1e-05
FAR_SCORE = -1000000000.0
MASK_PENALTY = 4.0


def passed_along(shard, axis, by):
    size = lax.axis_size(axis)
    return lax.ppermute(shard, axis, [(i, (i + by) % size) for i in range(size)])


def swapped(shard, axis, apart):
    return lax.ppermute(shard, axis, [(i, i ^ 1 << apart) for i in range(lax.axis_size(axis))])


def for_sending(shard):

    def short(part):
        return part.astype(jnp.bfloat16) if part.dtype == jnp.float32 else part

    return jax.tree.map(short, shard)


def norm_rows(values):
    wide = values.astype(jnp.float32)
    centre = jnp.mean(wide, axis=-1, keepdims=True)
    spread = jnp.mean(jnp.square(wide - centre), axis=-1, keepdims=True)
    return ((wide - centre) * lax.rsqrt(spread + NORM_EPS)).astype(jnp.bfloat16)


def project(values, weight):
    flat_rows = values.reshape(-1, values.shape[-1])
    product = jnp.dot(flat_rows, weight, preferred_element_type=jnp.float32)
    return product.astype(jnp.bfloat16).reshape(values.shape[:-1] + (weight.shape[1],))


def add_round(first, second):
    return (first.astype(jnp.float32) + second.astype(jnp.float32)).astype(jnp.bfloat16)


def attend(query, key_rows, value_rows, bias):
    score_scale = query.shape[-1] ** (-0.5)
    scores = (
        jnp.einsum("bqhd,bkhd->bhqk", query, key_rows, preferred_element_type=jnp.float32)
        * score_scale
    )
    scores = scores + bias[:, None]
    row_peak = jnp.max(scores, axis=-1, keepdims=True)
    expo = jnp.exp(scores - row_peak)
    softmax_w = (expo / jnp.sum(expo, axis=-1, keepdims=True)).astype(jnp.bfloat16)
    mixed = jnp.einsum("bhqk,bkhd->bqhd", softmax_w, value_rows, preferred_element_type=jnp.float32)
    return mixed.astype(jnp.bfloat16)


def to_windows(values, win_levels, win_rows, win_cols):
    levels, lat_rows, lon_cols = values.shape[:3]
    trailing = values.shape[3:]
    values = values.reshape(
        (
            levels // win_levels,
            win_levels,
            lat_rows // win_rows,
            win_rows,
            lon_cols // win_cols,
            win_cols,
        )
        + trailing
    )
    perm_axes = (0, 2, 4, 1, 3, 5) + tuple(range(6, 6 + len(trailing)))
    values = jnp.transpose(values, perm_axes)
    count = levels // win_levels * (lat_rows // win_rows) * (lon_cols // win_cols)
    return values.reshape((count, win_levels * win_rows * win_cols) + trailing)


def from_windows(windows, levels, lat_rows, lon_cols, win_levels, win_rows, win_cols):
    trailing = windows.shape[2:]
    windows = windows.reshape(
        (
            levels // win_levels,
            lat_rows // win_rows,
            lon_cols // win_cols,
            win_levels,
            win_rows,
            win_cols,
        )
        + trailing
    )
    perm_axes = (0, 3, 1, 4, 2, 5) + tuple(range(6, 6 + len(trailing)))
    return jnp.transpose(windows, perm_axes).reshape((levels, lat_rows, lon_cols) + trailing)


def window_mix(query_in, kv_in, bias):
    levels, lat_rows, lon_cols, channels = query_in.shape
    heads = channels // HD
    key_cols = kv_in.shape[2]
    query = to_windows(
        query_in.reshape(levels, lat_rows, lon_cols, heads, HD), WLEV, WLAT, lon_cols
    )
    kv_win = to_windows(
        kv_in.reshape(levels, lat_rows, key_cols, 2, heads, HD), WLEV, WLAT, key_cols
    )
    mixed = attend(query, kv_win[:, :, 0], kv_win[:, :, 1], bias)
    return from_windows(mixed, levels, lat_rows, lon_cols, WLEV, WLAT, lon_cols).reshape(
        levels, lat_rows, lon_cols, channels
    )


def merge_block(fine, w_merge):
    levels, lat_rows, lon_cols, channels = fine.shape
    grouped = fine.reshape(levels, lat_rows // 2, 2, lon_cols // 2, 2, channels)
    grouped = jnp.transpose(grouped, (0, 1, 3, 2, 4, 5)).reshape(
        levels, lat_rows // 2, lon_cols // 2, 4 * channels
    )
    return project(norm_rows(grouped), w_merge)


def tail_block(fine, deeper, w_up):
    upward = project(deeper, w_up)
    spread_up = jnp.repeat(jnp.repeat(upward, 2, axis=1), 2, axis=2)
    return add_round(fine, spread_up)


def roll_in(field):
    left_edge = field
    arrived = passed_along(left_edge, "lon", -1)
    field = jnp.concatenate([field[:, :, SHLON:], arrived], axis=2)
    top_rows = field[:, :SHLAT]
    arrived = passed_along(top_rows, "lat", -1)
    return jnp.concatenate([field[:, SHLAT:], arrived], axis=1)


def roll_out(field):
    bottom_rows = field[:, -SHLAT:]
    arrived = passed_along(bottom_rows, "lat", 1)
    field = jnp.concatenate([arrived, field[:, : field.shape[1] - SHLAT]], axis=1)
    arrived = passed_along(field, "lon", 1)
    return jnp.concatenate([arrived, field[:, :, : field.shape[2] - SHLON]], axis=2)


def order_pair(own_part, other_part, is_first):
    first_half = jnp.where(is_first, own_part, other_part)
    second_half = jnp.where(is_first, other_part, own_part)
    return jnp.concatenate([first_half, second_half], axis=2)


def split_pair(joined, is_first):
    half_cols = joined.shape[2] // 2
    first_half = joined[:, :, :half_cols]
    second_half = joined[:, :, half_cols:]
    return (
        jnp.where(is_first, first_half, second_half),
        jnp.where(is_first, second_half, first_half),
    )


def quad_gather(values, mask, is_even, is_low):
    near_values, near_mask = swapped((values, mask), "lon", 0)
    pair_values = order_pair(values, near_values, is_even)
    pair_mask = order_pair(mask, near_mask, is_even)
    far_values, far_mask = (
        swapped(pair_values, "lon", 1),
        swapped(for_sending(pair_mask), "lon", 1).astype(pair_mask.dtype),
    )
    return (order_pair(pair_values, far_values, is_low), order_pair(pair_mask, far_mask, is_low))


def quad_return(grad_quad, is_even, is_low):
    own_pair, far_pair = split_pair(grad_quad, is_low)
    pair_grad = own_pair + swapped(far_pair, "lon", 1)
    own_part, near_part = split_pair(pair_grad, is_even)
    return own_part + swapped(near_part, "lon", 0)


MESH = pl.DeviceIdType.MESH
NZ = 8
NY = 4
WEIGHT_COUNT = 5


def place():
    lon, lat = lax.axis_index("lon"), lax.axis_index("lat")
    return lon // (2 * NY), lon // 2 % NY, lon % 2, lat // 2, lat % 2


def gather_kernel(*refs):
    own = refs[:WEIGHT_COUNT]
    full = refs[WEIGHT_COUNT : 2 * WEIGHT_COUNT]
    send_sems, recv_sems, local_sems = refs[2 * WEIGHT_COUNT :]
    z, y, c, x, y_hi = place()

    def at(dz, dy, flip=False):
        row = y + dy + NY
        carried = (y_hi + row // NY + 1) % 2
        core = 1 - c if flip else c
        return {
            "lon": ((z + dz + NZ) % NZ * NY + row % NY) * 2 + core,
            "lat": x * 2 + carried,
        }

    z_at = lambda dz: (z + dz + NZ) % NZ
    y_at = lambda dy: (y + dy + NY) % NY
    up_z, down_z, up_y, down_y, twin = at(1, 0), at(-1, 0), at(0, 1), at(0, -1), at(0, 0, True)

    barrier = pltpu.get_barrier_semaphore()
    for peer in (up_z, down_z, up_y, down_y, twin):
        pl.semaphore_signal(barrier, inc=1, device_id=peer, device_id_type=MESH)
    pl.semaphore_wait(barrier, 5)

    locals_ = [
        pltpu.make_async_copy(own[k], full[k].at[z, y, c], local_sems.at[k])
        for k in range(WEIGHT_COUNT)
    ]
    for copy in locals_:
        copy.start()

    started = []

    def send(source, target, peer):
        index = len(started)
        copy = pltpu.make_async_remote_copy(
            src_ref=source,
            dst_ref=target,
            send_sem=send_sems.at[index],
            recv_sem=recv_sems.at[index],
            device_id=peer,
            device_id_type=MESH,
        )
        copy.start()
        started.append(copy)
        return copy

    def pass_on(view, peer):
        return send(view, view, peer)

    def arrived(copies):
        for copy in copies:
            copy.wait_recv()

    first, second = (0, 1, 2), (3, 4)
    twin_copies = []

    def to_twin(k, where):
        twin_copies.append(pass_on(full[k].at[where], twin))

    here = lambda k: full[k].at[z, y, c]
    near = [[send(own[k], here(k), peer) for k in second] for peer in (up_y, down_y)]
    ring = {}
    ring[1] = [[send(own[k], here(k), peer) for k in first] for peer in (up_z, down_z)]
    across = {0: [[send(own[k], here(k), peer) for k in first] for peer in (up_y, down_y)]}

    half_cut = {3: (pl.ds(0, 16), pl.ds(16, 16)), 4: (pl.ds(0, 256), pl.ds(256, 256))}

    def half_of(k, dz, dy, which):
        cut = half_cut[k][which]
        spot = full[k].at[z_at(dz), y_at(dy), c]
        return spot.at[cut] if k == 3 else spot.at[:, cut]

    arrived(near[0])
    far = [[pass_on(half_of(k, 0, -1, 0), up_y) for k in second]]
    arrived(near[1])
    far.append([pass_on(half_of(k, 0, 1, 1), down_y) for k in second])

    def forward_first(step):
        arrived(ring[step][0])
        arrived(ring[step][1])
        spots = [lambda k, d=d: full[k].at[z_at(d), y, c] for d in (-step, step)]
        if step < 3:
            ring[step + 1] = [
                [pass_on(spot(k), peer) for k in first] for spot, peer in zip(spots, (up_z, down_z))
            ]
        elif step == 3:
            ring[4] = [
                [
                    pass_on(spots[0](0).at[:, pl.ds(0, 1536)], up_z),
                    pass_on(spots[0](1), up_z),
                ],
                [
                    pass_on(spots[1](0).at[:, pl.ds(1536, 1536)], down_z),
                    pass_on(spots[1](2), down_z),
                ],
            ]
        for d, spot in ((-step, spots[0]), (step, spots[1]))[: 2 if step < 4 else 1]:
            across[d % NZ] = [[pass_on(spot(k), peer) for k in first] for peer in (up_y, down_y)]

    forward_first(1)
    arrived(far[0])
    arrived(far[1])
    for copy in locals_:
        copy.wait()
    wheel = {
        1: [[pass_on(full[k].at[z, :, c], peer) for k in second] for peer in (up_z, down_z)]
    }
    for k in second:
        to_twin(k, (z, slice(None), c))
    forward_first(2)
    forward_first(3)
    forward_first(4)
    for k in first:
        to_twin(k, (slice(None), y, c))

    def forward_second(step):
        arrived(wheel[step][0])
        arrived(wheel[step][1])
        if step < 3:
            wheel[step + 1] = [
                [pass_on(full[k].at[z_at(d), :, c], peer) for k in second]
                for d, peer in ((-step, up_z), (step, down_z))
            ]
        elif step == 3:
            wheel[4] = [
                [pass_on(full[k].at[z_at(d), pl.ds(cut, 2), c], peer) for k in second]
                for d, cut, peer in ((-step, 0, up_z), (step, 2, down_z))
            ]
        for d in (-step, step)[: 2 if step < 4 else 1]:
            for k in second:
                to_twin(k, (z_at(d), slice(None), c))

    last = []

    def spread(dz, turn):
        arrived(across[dz][0])
        arrived(across[dz][1])
        if turn % 2 == 0:
            last.append([pass_on(full[k].at[z_at(dz), y_at(-1), c], up_y) for k in first])
        else:
            last.append([pass_on(full[k].at[z_at(dz), y_at(1), c], down_y) for k in first])

    order = (0, 7, 1, 6, 2, 5, 3, 4)
    spread(order[0], 0)
    spread(order[1], 1)
    forward_second(1)
    spread(order[2], 0)
    spread(order[3], 1)
    forward_second(2)
    spread(order[4], 0)
    spread(order[5], 1)
    forward_second(3)
    spread(order[6], 0)
    spread(order[7], 1)
    for k in first:
        to_twin(k, (slice(None), y_at(1), c))
        to_twin(k, (slice(None), y_at(-1), c))
    forward_second(4)
    for copies in last:
        arrived(copies)
    for k in first:
        to_twin(k, (slice(None), y_at(2), c))
    arrived(twin_copies)
    for copy in started:
        copy.wait_send()


GATHER_COPIES = 200


def gather_weights(w_fine_qkv, w_fine_out, w_merge, w_coarse_qkv, w_up):
    shards = (w_coarse_qkv, w_fine_qkv, w_fine_out, w_merge, w_up)
    anywhere = pl.BlockSpec(memory_space=pl.ANY)
    full = pl.pallas_call(
        gather_kernel,
        out_shape=[jax.ShapeDtypeStruct((NZ, NY, 2) + w.shape, w.dtype) for w in shards],
        in_specs=[anywhere] * WEIGHT_COUNT,
        out_specs=[anywhere] * WEIGHT_COUNT,
        scratch_shapes=[
            pltpu.SemaphoreType.DMA((GATHER_COPIES,)),
            pltpu.SemaphoreType.DMA((GATHER_COPIES,)),
            pltpu.SemaphoreType.DMA((WEIGHT_COUNT,)),
        ],
        compiler_params=pltpu.CompilerParams(collective_id=0, has_side_effects=True),
    )(*shards)
    coarse, fine_qkv, fine_out, merge, up = [
        f.reshape((NZ * NY * 2 * w.shape[0], w.shape[1])) for f, w in zip(full, shards)
    ]
    return fine_qkv, fine_out, merge, coarse, up


def body(fields, w_fine_qkv, w_fine_out, w_merge, w_coarse_qkv, w_up, coarse_mask, cotangent):
    coarse_width = w_coarse_qkv.shape[1] // 3
    full_fq, full_fo, full_m, full_cq, full_up = gather_weights(
        w_fine_qkv, w_fine_out, w_merge, w_coarse_qkv, w_up
    )
    w_query = full_cq[:, :coarse_width]
    w_pair = full_cq[:, coarse_width:]
    levels, lat_rows, lon_cols, fine_width = fields.shape
    lat_index = lax.axis_index("lat") * lat_rows + jnp.arange(lat_rows)
    seam_rows = lat_index >= lat_rows * lax.axis_size("lat") - SHLAT
    lon_index = lax.axis_index("lon")
    is_even = lon_index % 2 == 0
    is_low = lon_index // 2 % 2 == 0
    query_region = jnp.broadcast_to(seam_rows[None, :, None], (levels, lat_rows, lon_cols)).astype(
        jnp.float32
    )
    key_region = jnp.broadcast_to(
        seam_rows[None, :, None], (levels, lat_rows, 2 * lon_cols)
    ).astype(jnp.float32)
    query_win = to_windows(query_region, WLEV, WLAT, lon_cols)
    key_win = to_windows(key_region, WLEV, WLAT, 2 * lon_cols)
    fine_bias = jnp.where(
        query_win[:, :, None] == key_win[:, None, :], jnp.float32(0.0), jnp.float32(FAR_SCORE)
    )

    def fine_front(rolled):
        qkv = project(norm_rows(rolled), full_fq)
        return (qkv[..., :fine_width], qkv[..., fine_width:])

    def fine_core(query_in, pair_kv):
        return project(window_mix(query_in, pair_kv, fine_bias), full_fo)

    def merge_apply(skip):
        return merge_block(skip, full_m)

    def tail_apply(skip, deeper):
        return tail_block(skip, deeper, full_up)

    rolled = roll_in(fields)
    (fine_query, own_kv), front_pull = jax.vjp(fine_front, rolled)
    other_kv = swapped(own_kv, "lon", 0)
    pair_kv = order_pair(own_kv, other_kv, is_even)
    mixed_rolled, core_pull = jax.vjp(fine_core, fine_query, pair_kv)
    skip = add_round(fields, roll_out(mixed_rolled))
    coarse, merge_pull = jax.vjp(merge_apply, skip)
    normed, norm_pull = jax.vjp(norm_rows, coarse)
    quad_normed, quad_mask = quad_gather(normed, coarse_mask, is_even, is_low)
    mask_win = to_windows(quad_mask.astype(jnp.float32), WLEV, WLAT, quad_mask.shape[2])
    quad_bias = (-MASK_PENALTY * (1.0 - mask_win))[:, None, :]

    def coarse_apply(residual_in, own_normed, all_normed):
        query_in = project(own_normed, w_query)
        kv_in = project(all_normed, w_pair)
        return add_round(residual_in, window_mix(query_in, kv_in, quad_bias))

    deeper, coarse_pull = jax.vjp(coarse_apply, coarse, normed, quad_normed)
    output, tail_pull = jax.vjp(tail_apply, skip, deeper)
    grad_skip_tail, grad_deeper = tail_pull(cotangent)
    grad_residual, grad_own, grad_all = coarse_pull(grad_deeper)
    grad_normed = grad_own + quad_return(grad_all, is_even, is_low)
    (grad_norm_in,) = norm_pull(grad_normed)
    grad_coarse = grad_residual + grad_norm_in
    (grad_skip_merge,) = merge_pull(grad_coarse)
    grad_skip = grad_skip_tail + grad_skip_merge
    grad_query, grad_pair = core_pull(roll_in(grad_skip))
    own_grad, other_grad = split_pair(grad_pair, is_even)
    grad_kv = own_grad + swapped(other_grad, "lon", 0)
    (grad_rolled,) = front_pull((grad_query, grad_kv))
    grad_fields = grad_skip + roll_out(grad_rolled)
    return (output, grad_fields)


def solution(mesh):
    placed = (
        P(None, "lat", "lon", None),
        P("lon", None),
        P("lon", None),
        P("lon", None),
        P("lon", None),
        P("lon", None),
        P(None, "lat", "lon"),
        P(None, "lat", "lon", None),
    )
    return jax.shard_map(
        body,
        mesh=mesh,
        in_specs=placed,
        out_specs=(P(None, "lat", "lon", None), P(None, "lat", "lon", None)),
        check_vma=False,
    )
```

```python
import functools
from types import SimpleNamespace

import jax
import jax.numpy as jnp
import ml_dtypes
import numpy as np
from jax import lax
from jax.experimental import pallas as pl
from jax.experimental.pallas import tpu as pltpu
from jax.sharding import PartitionSpec as P

HD = 32
SHLAT = 3
NORM_EPS = 1e-05
FAR_SCORE = -1000000000.0
MASK_PENALTY = 4.0

MESH = pl.DeviceIdType.MESH
OWN = 144
HALO = 48
HALO_REAL = 36
REAL_KEYS = 2 * OWN + 4 * HALO
KEYS = 512
DEPTH = 256
CROWS = 48
CREAL = 36
REAL_CKEYS = 4 * CROWS
CKEYS = 256
FINE = 512
COARSE = 1024
GROUP = 256
HEADS = 8
LEVELS, LAT_ROWS, LON_COLS = 2, 12, 6
LEVEL = LAT_ROWS * LON_COLS


def constants():
    token = np.arange(OWN)
    level, row, col = token // 72, token // 6 % 12, token % 6
    pick = np.zeros((4 * CROWS, OWN), np.float32)
    coarse_at = level * 18 + row // 2 * 3 + col // 2
    pick[(row % 2 * 2 + col % 2) * CROWS + coarse_at, token] = 1
    shrink = pick.reshape(4, CROWS, OWN).sum(0)
    edge = np.zeros((OWN, 4 * HALO), np.float32)
    for slot in range(4):
        low = 9 if slot < 2 else 0
        inside = (row >= low) & (row < low + 3)
        edge[token[inside], slot * HALO + (level * 18 + (row - low) * 6 + col)[inside]] = 1
    bands = np.zeros((8, KEYS), np.float32)
    bands[0] = -1
    own_band = np.where(row < 3, 0, np.where(row < 9, 1, 2))
    bands[0, :OWN] = own_band
    bands[0, OWN : 2 * OWN] = own_band
    for slot in range(4):
        start = 2 * OWN + slot * HALO
        bands[0, start : start + HALO_REAL] = 0 if slot < 2 else 2
        bands[1 + slot // 2, start : start + HALO] = 10
    own_bands = np.zeros((OWN, 128), np.float32) + own_band[:, None]
    rims = np.zeros((2 * HALO, OWN), np.float32)
    for start, low in ((0, 0), (HALO, 9)):
        inside = (row >= low) & (row < low + 3)
        rims[start + (level * 18 + (row - low) * 6 + col)[inside], token[inside]] = 1
    entry = np.arange(CREAL)
    mask_place = np.zeros((18, LEVELS, GROUP), np.float32)
    mask_place[entry % 18, entry // 18, entry] = 1

    def deep(a, depth=DEPTH):
        return np.pad(a, ((0, 0), (0, depth - a.shape[1])))

    return (
        deep(pick), deep(pick.T), deep(shrink), deep(shrink.T, 128), deep(edge),
        deep(rims), bands, own_bands, mask_place,
    )


def mm(a, b):
    return lax.dot_general(a, b, (((1,), (0,)), ((), ())), preferred_element_type=jnp.float32)


def mt(a, b):
    return lax.dot_general(a, b, (((1,), (1,)), ((), ())), preferred_element_type=jnp.float32)


def tm(a, b):
    return lax.dot_general(a, b, (((0,), (0,)), ((), ())), preferred_element_type=jnp.float32)


def short(a):
    return a.astype(jnp.bfloat16)


def wide(a):
    return a.astype(jnp.float32)


def deepened(a, depth=DEPTH):
    return jnp.concatenate([a, jnp.zeros((depth - a.shape[0], a.shape[1]), a.dtype)], axis=0)


def normed_rows(values):
    centre = jnp.mean(values, axis=-1, keepdims=True)
    off = values - centre
    inverse = lax.rsqrt(jnp.mean(off * off, axis=-1, keepdims=True) + NORM_EPS)
    return off * inverse, inverse


def norm_pull(values, grad):
    hat, inverse = normed_rows(values)
    along = jnp.mean(grad * hat, axis=-1, keepdims=True)
    return inverse * (grad - jnp.mean(grad, axis=-1, keepdims=True) - hat * along)


def head_lanes(head):
    return lax.broadcasted_iota(jnp.int32, (1, GROUP), 1) // HD == head


def stack_heads(target, block):
    rows = block.shape[0]
    for head in range(HEADS):
        target[pl.ds(head * rows, rows), :] = jnp.where(
            head_lanes(head), block, jnp.zeros_like(block)
        )


def join_heads(stacked, rows):
    total = jnp.where(head_lanes(0), stacked[:rows], 0.0)
    for head in range(1, HEADS):
        total = total + jnp.where(
            head_lanes(head), stacked[head * rows : (head + 1) * rows], 0.0
        )
    return short(total)


def blocks(count, step):
    def one(index, carry):
        step(index)
        return carry

    lax.fori_loop(0, count, one, 0)


def wide_columns(index, start=0, size=GROUP):
    return pl.ds(pl.multiple_of(start + index * size, size), size)


def lanes(group, start=0):
    if isinstance(group, int):
        return pl.ds(start + group * GROUP, GROUP)
    return pl.ds(pl.multiple_of(start + group * GROUP, GROUP), GROUP)


def attend(rows, channels, q, kv, bias, out, stack, scores, weights, pump):
    together = rows if rows >= OWN else HEADS * rows

    def one_group(group):
        stack_heads(stack, q[:, lanes(group)])
        scores[...] = mt(stack[...], kv[:, lanes(group)])
        if pump is not None:
            pump()

        def one_head(head, carry):
            spot = pl.ds(pl.multiple_of(head * together, 16), together)
            s = scores[spot, :] * (HD**-0.5) + bias[...]
            e = jnp.exp(s - jnp.max(s, axis=-1, keepdims=True))
            weights[group, spot, :] = short(e * (1.0 / jnp.sum(e, axis=-1, keepdims=True)))
            return carry

        lax.fori_loop(0, HEADS * rows // together, one_head, 0, unroll=4 if together == rows else 1)
        if pump is not None:
            pump()
        out[:, lanes(group)] = join_heads(mm(weights[group], kv[:, lanes(group, channels)]), rows)
        if pump is not None:
            pump()

    if pump is None:
        blocks(channels // GROUP, one_group)
    else:
        for group in range(channels // GROUP):
            one_group(group)


def attend_pull(rows, channels, q, kv, grad, dq, dkv, stack, scores, weights, inner):
    together = rows if rows >= OWN else HEADS * rows

    def one_group(group, carry):
        stack_heads(stack, grad[:, lanes(group)])
        scores[...] = mt(stack[...], kv[:, lanes(group, channels)])

        def one_head(head, carry):
            spot = pl.ds(pl.multiple_of(head * together, 16), together)
            p = wide(weights[group, spot, :])
            d = scores[spot, :]
            mean = jnp.sum(p * d, axis=-1, keepdims=True)
            inner[spot, :] = short(p * (d - mean) * (HD**-0.5))
            return carry

        lax.fori_loop(0, HEADS * rows // together, one_head, 0, unroll=4 if together == rows else 1)
        dkv[:, lanes(group, channels)] = short(tm(weights[group], stack[...]))
        dq[:, lanes(group)] = join_heads(mm(inner[...], kv[:, lanes(group)]), rows)
        stack_heads(stack, q[:, lanes(group)])
        dkv[:, lanes(group)] = short(tm(inner[...], stack[...]))
        return carry

    lax.fori_loop(0, channels // GROUP, one_group, 0)


def exchange_peers(size_lon, size_lat):
    lon, lat = lax.axis_index("lon"), lax.axis_index("lat")
    odd = lon % 2
    at = lambda lon_at, lat_at: {"lon": lon_at, "lat": lat_at}
    mate = (lon + 2 * odd - 1 + size_lon) % size_lon
    before, after = (lat + size_lat - 1) % size_lat, (lat + 1) % size_lat
    near = lon + 1 - 2 * odd
    step = 2 - 4 * (lon // 2 % 2)
    return SimpleNamespace(
        mate=at(mate, lat),
        before=at(lon, before),
        before_mate=at(mate, before),
        after=at(lon, after),
        after_mate=at(mate, after),
        quad=(at(near, lat), at(lon + step, lat), at(near + step, lat)),
        first=jnp.where(lat == 0, 1.0, 0.0),
        last=jnp.where(lat == size_lat - 1, 1.0, 0.0),
    )


def layer_scratch():
    bf = lambda *s: pltpu.VMEM(s, jnp.bfloat16)
    f32 = lambda *s: pltpu.VMEM(s, jnp.float32)
    return dict(
        xk=bf(KEYS, FINE), masks=f32(4, 8, GROUP),
        kn=bf(4, CROWS, COARSE), dn_send=bf(3, CROWS, COARSE), dn_got=bf(3, CROWS, COARSE),
        df_send=bf(KEYS, FINE), mate_got=bf(OWN, FINE), halo_got=bf(DEPTH, FINE),
        fq=bf(OWN, FINE), fkv=bf(KEYS, 2 * FINE), fbias=f32(OWN, KEYS), mixed=bf(OWN, FINE),
        fstack=bf(HEADS * OWN, GROUP), fscores=f32(HEADS * OWN, KEYS),
        fweights=bf(FINE // GROUP, HEADS * OWN, KEYS), finner=bf(HEADS * OWN, KEYS),
        dmix=bf(OWN, FINE), dfq=bf(OWN, FINE), dfkv=bf(KEYS, 2 * FINE),
        cq=bf(CROWS, COARSE), ckv=bf(CKEYS, 2 * COARSE), cbias=f32(1, CKEYS),
        cmixed=bf(CROWS, COARSE),
        cstack=bf(HEADS * CROWS, GROUP), cscores=f32(HEADS * CROWS, CKEYS),
        cweights=bf(COARSE // GROUP, HEADS * CROWS, CKEYS), cinner=bf(HEADS * CROWS, CKEYS),
        ddeep=bf(CROWS, COARSE), dcq=bf(CROWS, COARSE), dckv=bf(CKEYS, 2 * COARSE),
        skip=bf(OWN, FINE), coarse=bf(CROWS, COARSE), grad_skip=bf(OWN, FINE),
        grouped=bf(CROWS, 4 * FINE), mask_send=f32(4, 8, GROUP), x_in=bf(OWN + 2 * HALO, FINE),
        cot=bf(OWN, FINE),
        w_fq=bf(FINE, 3 * FINE), w_fo=bf(FINE, FINE), xn=bf(KEYS, FINE),
        group_normed=bf(CROWS, 4 * FINE), d_group=f32(CROWS, 4 * FINE),
        d_normed=f32(CROWS, COARSE), d_fine=f32(OWN, FINE), deeper=bf(CROWS, COARSE),
        d_up=bf(CROWS, FINE), d_coarse=bf(CROWS, COARSE), upward=bf(CROWS, FINE),
        fine_mixed=bf(OWN, FINE),
    )


COPIES = 224


def unpack(field, target):
    both = wide(field[...])
    for level in range(LEVELS):
        target[pl.ds(level * LEVEL, LEVEL), :] = short(both[:, level, :])


def pack(values, target):
    halves = [values[level * LEVEL : (level + 1) * LEVEL] for level in range(LEVELS)]
    target[...] = short(jnp.stack(halves, axis=1))


def layer(peers, send, steps, field, cot_field, mask_field, consts, out, grad_out, full, ready, s):
    pick, pick_t, shrink, spread, edge, rims, bands, own_bands, mask_place = consts

    def pump(count=1):
        for _ in range(count):
            next(steps, None)

    def need(name):
        while name not in ready:
            next(steps, None)

    def columns_of(name, index, start=0):
        if name == FQ:
            return s.w_fq[:, wide_columns(index, start)]
        if name == FO:
            return s.w_fo[:, wide_columns(index, start)]
        return full[name][:, :, :, :, wide_columns(index, start)].reshape(-1, GROUP)

    def rows_of(name, index, columns=slice(None)):
        if name in (FQ, FO):
            rows = pl.ds(pl.multiple_of(index * GROUP, GROUP), GROUP)
            return (s.w_fq if name == FQ else s.w_fo)[rows, columns]
        slabs = GROUP // (2 * NY * full[name].shape[3])
        part = full[name][pl.ds(index * slabs, slabs), :, :, :, columns]
        return part.reshape(GROUP, part.shape[-1])

    def project(target, source, name, start=0):
        need(name)

        def step(index):
            target[:, wide_columns(index)] = short(mm(source[...], columns_of(name, index, start)))

        blocks(target.shape[-1] // GROUP, step)

    x_in, cot = s.x_in, s.cot
    unpack(field, x_in)
    rim_rows = mm(short(rims[...]), deepened(x_in[pl.ds(0, OWN), :]))
    x_in[pl.ds(OWN, 2 * HALO), :] = short(rim_rows)
    mask_row = jnp.zeros((1, GROUP), jnp.float32)
    for col in range(3):
        entries = -MASK_PENALTY * (1.0 - mask_field[col].astype(jnp.float32))
        for row in range(6):
            placed = entries[:, row : row + 1] * mask_place[row * 3 + col]
            mask_row = mask_row + jnp.sum(placed, axis=0, keepdims=True)
    lane = lax.broadcasted_iota(jnp.int32, (1, GROUP), 1)
    absent = (lane >= CREAL) & (lane < CROWS)
    mask_row = jnp.broadcast_to(jnp.where(absent, FAR_SCORE, mask_row), (8, GROUP))
    mask_in, masks = s.mask_send, s.masks
    mask_in[0] = mask_row
    for j in range(1, 4):
        mask_in[j] = pltpu.roll(mask_row, j * CROWS, 1)

    xk = s.xk
    top, bottom = x_in.at[pl.ds(OWN, HALO)], x_in.at[pl.ds(OWN + HALO, HALO)]
    slot = lambda ref, i: ref.at[pl.ds(2 * OWN + i * HALO, HALO)]
    opening = [
        send(x_in.at[pl.ds(0, OWN)], xk.at[pl.ds(OWN, OWN)], peers.mate),
        send(bottom, slot(xk, 0), peers.after),
        send(bottom, slot(xk, 1), peers.after_mate),
        send(top, slot(xk, 2), peers.before),
        send(top, slot(xk, 3), peers.before_mate),
    ]
    mask_copies = [
        send(mask_in.at[j + 1], masks.at[j + 1], peers.quad[j]) for j in range(3)
    ]
    pump(2)
    xk[pl.ds(0, OWN), :] = x_in[pl.ds(0, OWN), :]
    xk[pl.ds(REAL_KEYS, KEYS - REAL_KEYS), :] = jnp.zeros((KEYS - REAL_KEYS, FINE), jnp.bfloat16)
    halo_got = s.halo_got
    halo_got[pl.ds(4 * HALO, DEPTH - 4 * HALO), :] = jnp.zeros((DEPTH - 4 * HALO, FINE), jnp.bfloat16)
    masks[0] = mask_in[0]
    key_bands = bands[0:1] + peers.first * bands[1:2] + peers.last * bands[2:3]
    s.fbias[...] = jnp.where(own_bands[:, 0:1] == key_bands, 0.0, FAR_SCORE)
    pump(2)
    unpack(cot_field, cot)
    pump(2)
    for copy in opening:
        copy.wait_recv()

    def norm_step(index):
        rows = pl.ds(pl.multiple_of(index * 128, 128), 128)
        s.xn[rows, :] = short(normed_rows(wide(xk[rows, :]))[0])

    blocks(KEYS // 128, norm_step)
    pump(2)
    project(s.fq, s.xn.at[pl.ds(0, OWN)], FQ)
    pump()
    project(s.fkv, s.xn, FQ, FINE)
    pump()
    attend(OWN, FINE, s.fq, s.fkv, s.fbias, s.mixed, s.fstack, s.fscores, s.fweights, pump)
    project(s.fine_mixed, s.mixed, FO)
    pump()
    skip = short(wide(x_in[pl.ds(0, OWN), :]) + wide(s.fine_mixed[...]))
    s.skip[...] = skip

    picked = short(mm(short(pick[...]), deepened(skip)))
    for part in range(4):
        s.grouped[:, pl.ds(part * FINE, FINE)] = picked[part * CROWS : (part + 1) * CROWS]
    s.group_normed[...] = short(normed_rows(wide(s.grouped[...]))[0])
    pump()
    project(s.coarse, s.group_normed, MG)
    kn = s.kn
    kn[0] = short(normed_rows(wide(s.coarse[...]))[0])
    quad_copies = [send(kn.at[0], kn.at[j + 1], peers.quad[j]) for j in range(3)]

    cot_here = cot[...]
    s.d_up[...] = short(mm(short(shrink[...]), deepened(cot_here)))
    need(UP)

    def up_step(index):
        s.ddeep[:, wide_columns(index)] = short(mt(s.d_up[...], rows_of(UP, index)))

    blocks(COARSE // GROUP, up_step)
    project(s.cq, kn.at[0], CQ)
    for copy in mask_copies + quad_copies:
        copy.wait_recv()
    total_mask = masks[0] + masks[1] + masks[2] + masks[3]
    s.cbias[...] = jnp.where(lane >= REAL_CKEYS, FAR_SCORE, total_mask[:1, :CKEYS])

    def ckv_step(index):
        s.ckv[pl.ds(0, REAL_CKEYS), wide_columns(index)] = short(
            mm(kn[...].reshape(REAL_CKEYS, COARSE), columns_of(CQ, index, COARSE))
        )

    blocks(2 * COARSE // GROUP, ckv_step)
    s.ckv[pl.ds(REAL_CKEYS, CKEYS - REAL_CKEYS), :] = jnp.zeros(
        (CKEYS - REAL_CKEYS, 2 * COARSE), jnp.bfloat16
    )
    attend(CROWS, COARSE, s.cq, s.ckv, s.cbias, s.cmixed, s.cstack, s.cscores, s.cweights, None)
    s.deeper[...] = short(wide(s.coarse[...]) + wide(s.cmixed[...]))
    project(s.upward, s.deeper, UP)
    output = (wide(s.skip[...]) + mm(short(spread[...]), deepened(s.upward[...], 128)))
    pack(output, out)

    attend_pull(CROWS, COARSE, s.cq, s.ckv, s.ddeep, s.dcq, s.dckv, s.cstack, s.cscores, s.cweights, s.cinner)
    def all_step(index):
        at = wide_columns(index)
        d_all = mt(s.dckv[pl.ds(0, REAL_CKEYS), :], rows_of(CQ, index, pl.ds(COARSE, 2 * COARSE)))
        s.d_normed[:, at] = d_all[:CROWS]
        for j in range(3):
            s.dn_send[j, :, at] = short(d_all[(j + 1) * CROWS : (j + 2) * CROWS])

    blocks(COARSE // GROUP, all_step)
    back_copies = [
        send(s.dn_send.at[j], s.dn_got.at[j], peers.quad[j]) for j in range(3)
    ]

    def own_step(index):
        at = wide_columns(index)
        own_part = mt(s.dcq[...], rows_of(CQ, index, pl.ds(0, COARSE)))
        s.d_normed[:, at] = s.d_normed[:, at] + own_part

    blocks(COARSE // GROUP, own_step)
    for copy in back_copies:
        copy.wait_recv()
    d_normed = s.d_normed[...]
    for j in range(3):
        d_normed = d_normed + wide(s.dn_got[j])
    s.d_coarse[...] = short(wide(s.ddeep[...]) + norm_pull(wide(s.coarse[...]), d_normed))

    def merge_step(index):
        s.d_group[:, wide_columns(index)] = mt(s.d_coarse[...], rows_of(MG, index))

    blocks(4 * FINE // GROUP, merge_step)
    d_group = short(norm_pull(wide(s.grouped[...]), s.d_group[...]))
    d_picked = jnp.concatenate(
        [d_group[:, part * FINE : (part + 1) * FINE] for part in range(4)], axis=0
    )
    s.grad_skip[...] = short(wide(cot_here) + mm(short(pick_t[...]), deepened(d_picked)))

    def out_step(index):
        s.dmix[:, wide_columns(index)] = short(mt(s.grad_skip[...], rows_of(FO, index)))

    blocks(FINE // GROUP, out_step)
    attend_pull(OWN, FINE, s.fq, s.fkv, s.dmix, s.dfq, s.dfkv, s.fstack, s.fscores, s.fweights, s.finner)
    df_send = s.df_send

    def fine_step(index):
        at = wide_columns(index)
        df_all = mt(s.dfkv[...], rows_of(FQ, index, pl.ds(FINE, 2 * FINE)))
        s.d_fine[:, at] = df_all[:OWN]
        df_send[:, at] = short(df_all)

    blocks(FINE // GROUP, fine_step)
    halo_got = s.halo_got
    got = lambda i: halo_got.at[pl.ds(i * HALO, HALO)]
    end_copies = [
        send(df_send.at[pl.ds(OWN, OWN)], s.mate_got, peers.mate),
        send(slot(df_send, 0), got(0), peers.before),
        send(slot(df_send, 1), got(1), peers.before_mate),
        send(slot(df_send, 2), got(2), peers.after),
        send(slot(df_send, 3), got(3), peers.after_mate),
    ]

    def query_step(index):
        at = wide_columns(index)
        own_part = mt(s.dfq[...], rows_of(FQ, index, pl.ds(0, FINE)))
        s.d_fine[:, at] = s.d_fine[:, at] + own_part

    blocks(FINE // GROUP, query_step)
    for copy in end_copies:
        copy.wait_recv()
    d_fine = s.d_fine[...] + wide(s.mate_got[...])
    from_halo = s.fscores.at[pl.ds(0, OWN), :]
    from_halo[...] = mm(short(edge[...]), halo_got[...])
    d_fine = d_fine + from_halo[...]
    pulled = norm_pull(wide(x_in[pl.ds(0, OWN), :]), d_fine)
    pack(wide(s.grad_skip[...]) + pulled, grad_out)


NZ = 8
NY = 4
FQ, FO, MG, UP, CQ = range(5)
WEIGHTS = (FQ, FO, MG, UP, CQ)


def ring_peers():
    lon, lat = lax.axis_index("lon"), lax.axis_index("lat")
    z, y, c = lon // (2 * NY), lon // 2 % NY, lon % 2
    x, y_hi = lat // 2, lat % 2

    def at(dz, dy, core):
        row = y + dy + NY
        carried = (y_hi + row // NY + 1) % 2
        return {
            "lon": ((z + dz + NZ) % NZ * NY + row % NY) * 2 + core,
            "lat": x * 2 + carried,
        }

    peers = at(1, 0, c), at(-1, 0, c), at(0, 1, c), at(0, -1, c), at(0, 0, 1 - c)
    turn = jnp.where(x == 3, 1, -x)
    back = jnp.where(x == 3, -1, x)
    shift_core = jnp.where(x == 0, 1 - c, c)
    shift_to, shift_from = at(0, turn, shift_core), at(0, back, shift_core)
    along = [{"lon": lon, "lat": (x + d) % 4 * 2 + y_hi} for d in (1, 3)]
    rim = tuple(at(d, 0, c) for d in (2, -2, 3, -3, 4))
    return (x, y, z, c), peers + (*along, shift_to, shift_from) + rim


def gather_steps(spot, peers, own, full, send, local_sems, ready, s):
    x, y, z, c = spot
    up_z, down_z, up_y, down_y, twin, up_x, down_x, shift_to, _ = peers[:9]
    w = (x + y) % NY
    z_at = lambda dz: (z + dz + NZ) % NZ
    y_at = lambda dy: (y + dy + NY) % NY
    w_at = lambda dw: (w + dw + NY) % NY
    every = slice(None)
    here = lambda k: full[k].at[z, y, c]

    def arrived(copies):
        for copy in copies:
            copy.wait_recv()

    def pass_on(k, where, peer):
        view = full[k].at[where]
        return send(view, view, peer)

    def half(k, place, which):
        width = full[k].shape[-1] // 2
        return place + (every, pl.ds(which * width, width))

    twins = {name: [] for name in WEIGHTS}

    def to_twin(k, where):
        twins[k].append(pass_on(k, where, twin))

    locals_ = {}
    for index, k in enumerate(WEIGHTS):
        locals_[k] = pltpu.make_async_copy(own[k], here(k), local_sems.at[index])
        if k != CQ:
            locals_[k].start()

    near, far, wheel, ring, across = {}, {}, {}, {}, {}

    def yz_start(k):
        near[k] = [send(own[k], here(k), peer) for peer in (up_y, down_y)]

    def yz_far(k):
        arrived(near[k][:1])
        first = pass_on(k, half(k, (z, y_at(-1), c), 0), up_y)
        arrived(near[k][1:])
        far[k] = [first, pass_on(k, half(k, (z, y_at(1), c), 1), down_y)]

    def yz_round(k):
        arrived(far[k])
        locals_[k].wait()
        wheel[k] = [pass_on(k, (z, every, c), peer) for peer in (up_z, down_z)]
        to_twin(k, (z, every, c))

    def yz_step(k, step):
        arrived(wheel[k])
        if step < 3:
            wheel[k] = [
                pass_on(k, (z_at(-step), every, c), up_z),
                pass_on(k, (z_at(step), every, c), down_z),
            ]
        elif step == 3:
            wheel[k] = [
                pass_on(k, (z_at(-3), pl.ds(0, 2), c), up_z),
                pass_on(k, (z_at(3), pl.ds(2, 2), c), down_z),
            ]
        for d in (-step, step)[: 2 if step < 4 else 1]:
            to_twin(k, (z_at(d), every, c))

    def zy_start(k):
        ring[k] = [send(own[k], here(k), peer) for peer in (up_z, down_z)]

    def zy_step(k, step):
        arrived(ring[k])
        if step < 3:
            ring[k] = [
                pass_on(k, (z_at(-step), y, c), up_z),
                pass_on(k, (z_at(step), y, c), down_z),
            ]
        elif step == 3:
            ring[k] = [
                pass_on(k, half(k, (z_at(-3), y, c), 0), up_z),
                pass_on(k, half(k, (z_at(3), y, c), 1), down_z),
            ]

    def across_y(k, where):
        return [pass_on(k, (where, y, c), peer) for peer in (up_y, down_y)]

    def side(k):
        return (w_at, up_x, down_x) if k == CQ else (y_at, up_y, down_y)

    def chain_across(k, d):
        place, up, down = side(k)
        across[k, d % NZ] = [pass_on(k, (z_at(d), place(0), c), peer) for peer in (up, down)]

    def chain_step(k, step):
        place, _, _ = side(k)
        arrived(ring[k])
        if step < 3:
            ring[k] = [
                pass_on(k, (z_at(-step), place(0), c), up_z),
                pass_on(k, (z_at(step), place(0), c), down_z),
            ]
        elif step == 3:
            ring[k] = [
                pass_on(k, half(k, (z_at(-3), place(0), c), 0), up_z),
                pass_on(k, half(k, (z_at(3), place(0), c), 1), down_z),
            ]
        for d in (-step, step)[: 2 if step < 4 else 1]:
            chain_across(k, d)

    def chain_spread(k, dz, turn):
        place, up, down = side(k)
        arrived(across[k, dz])
        if turn == 0:
            last[k].append(pass_on(k, (z_at(dz), place(-1), c), up))
        else:
            last[k].append(pass_on(k, (z_at(dz), place(1), c), down))

    def chain_twins(k, offsets):
        place, _, _ = side(k)
        for d in offsets:
            to_twin(k, (every, place(d), c))

    last = {CQ: [], MG: []}
    shift = send(own[CQ], here(CQ), shift_to, wait_start=True)

    @pl.when(x == 0)
    def _():
        locals_[CQ].start()

    @pl.when(x > 0)
    def _():
        shift.start()

    fine = (FQ, FO)
    fine_z = [send(own[k], here(k), peer) for peer in (up_z, down_z) + peers[9:] for k in fine]
    ring[MG] = [send(own[MG], here(MG), peer) for peer in (up_z, down_z)]

    @pl.when(x == 0)
    def _():
        locals_[CQ].wait()

    @pl.when(x > 0)
    def _():
        shift.wait_recv()

    ring[CQ] = [pass_on(CQ, (z, w, c), peer) for peer in (up_z, down_z)]
    chain_across(CQ, 0)
    yield
    arrived(fine_z)
    fine_y = []
    for k in fine:
        locals_[k].wait()
        fine_y += across_y(k, every)
    for k in fine:
        to_twin(k, (every, y, c))
    across[MG, 0] = [send(own[MG], here(MG), peer) for peer in (up_y, down_y)]
    yz_start(UP)
    yield
    chain_step(CQ, 1)
    chain_step(MG, 1)
    yield
    chain_step(CQ, 2)
    chain_step(MG, 2)
    yield
    arrived(fine_y)
    fine_far = []
    for k in fine:
        fine_far += [
            pass_on(k, (pl.ds(0, 4), y_at(-1), c), up_y),
            pass_on(k, (pl.ds(4, 4), y_at(1), c), down_y),
        ]
    for k in fine:
        to_twin(k, (every, y_at(-1), c))
        to_twin(k, (every, y_at(1), c))
    chain_step(CQ, 3)
    chain_step(MG, 3)
    yz_far(UP)
    yield
    arrived(fine_far)
    for k in fine:
        to_twin(k, (every, y_at(2), c))
    chain_step(CQ, 4)
    chain_step(MG, 4)
    locals_[MG].wait()
    yield
    chain_spread(CQ, 0, 0)
    chain_spread(MG, 0, 0)
    chain_twins(CQ, (0,))
    chain_twins(MG, (0,))
    yz_round(UP)
    yield
    arrived(twins[FQ])

    def tidy(part):
        columns = wide_columns(part, 0, FINE)
        s.w_fq[:, columns] = short(wide(full[FQ][:, :, :, :, columns]).reshape(FINE, FINE))

    blocks(3, tidy)
    ready.add(FQ)
    chain_spread(CQ, 7, 1)
    chain_spread(MG, 7, 1)
    yield
    arrived(twins[FO])
    s.w_fo[...] = short(wide(full[FO][...]).reshape(FINE, FINE))
    ready.add(FO)
    chain_spread(CQ, 1, 0)
    chain_spread(MG, 1, 0)
    yield
    chain_spread(CQ, 6, 1)
    chain_spread(MG, 6, 1)
    yz_step(UP, 1)
    yield
    chain_spread(CQ, 2, 0)
    chain_spread(MG, 2, 0)
    yield
    chain_spread(CQ, 5, 1)
    chain_spread(MG, 5, 1)
    yz_step(UP, 2)
    yield
    chain_spread(CQ, 3, 0)
    chain_spread(MG, 3, 0)
    yield
    chain_spread(CQ, 4, 1)
    chain_spread(MG, 4, 1)
    chain_twins(MG, (-1, 1))
    chain_twins(CQ, (-1, 1))
    yz_step(UP, 3)
    yield
    arrived(last[MG])
    chain_twins(MG, (2,))
    yield
    arrived(last[CQ])
    chain_twins(CQ, (2,))
    yz_step(UP, 4)
    yield
    arrived(twins[MG])
    ready.add(MG)
    yield
    arrived(twins[CQ])
    ready.add(CQ)
    yield
    arrived(twins[UP])
    ready.add(UP)

    @pl.when(x > 0)
    def _():
        shift.wait_send()


def layer_kernel(size_lon, size_lat, names, *refs):
    field, cot_field, mask_field = refs[:3]
    consts, held = refs[3:12], refs[12:17]
    out, grad_out = refs[17:19]
    scratch = SimpleNamespace(**dict(zip(names, refs[19 : 19 + len(names)])))
    rest = refs[19 + len(names) :]
    full = dict(zip(WEIGHTS, rest[: len(WEIGHTS)]))
    send_sems, recv_sems, local_sems = rest[len(WEIGHTS) :]
    own = dict(zip(WEIGHTS, held))
    peers = exchange_peers(size_lon, size_lat)
    spot, rings = ring_peers()
    barrier = pltpu.get_barrier_semaphore()
    everyone = [peers.mate, peers.before, peers.before_mate, peers.after, peers.after_mate]
    everyone += list(peers.quad) + list(rings)
    for peer in everyone:
        pl.semaphore_signal(barrier, inc=1, device_id=peer, device_id_type=MESH)
    pl.semaphore_wait(barrier, len(everyone))
    started = []

    def send(source, target, peer, wait_start=False):
        index = len(started)
        assert index < COPIES
        copy = pltpu.make_async_remote_copy(
            src_ref=source, dst_ref=target, send_sem=send_sems.at[index],
            recv_sem=recv_sems.at[index], device_id=peer, device_id_type=MESH,
        )
        if not wait_start:
            copy.start()
        started.append(None if wait_start else copy)
        return copy

    ready = set()
    steps = gather_steps(spot, rings, own, full, send, local_sems, ready, scratch)
    layer(
        peers, send, steps, field, cot_field, mask_field, consts, out, grad_out, full, ready, scratch
    )
    for copy in started:
        if copy is not None:
            copy.wait_send()


def run_layer(mesh, fields, cotangent, coarse_mask, held):
    scratch = layer_scratch()
    vmem = pl.BlockSpec(memory_space=pltpu.VMEM)
    rows = (LEVEL, LEVELS, FINE)
    flat = lambda part: part.transpose(1, 2, 0, 3).reshape(rows)
    consts = constants()
    out, grad = pl.pallas_call(
        functools.partial(layer_kernel, mesh.shape["lon"], mesh.shape["lat"], tuple(scratch)),
        out_shape=[jax.ShapeDtypeStruct(rows, jnp.bfloat16)] * 2,
        in_specs=[vmem] * (3 + len(consts)) + [pl.BlockSpec(memory_space=pl.ANY)] * 5,
        out_specs=[vmem] * 2,
        scratch_shapes=list(scratch.values())
        + [pltpu.VMEM((NZ, NY, 2) + held[name].shape, jnp.bfloat16) for name in WEIGHTS]
        + [
            pltpu.SemaphoreType.DMA((COPIES,)),
            pltpu.SemaphoreType.DMA((COPIES,)),
            pltpu.SemaphoreType.DMA((len(WEIGHTS),)),
        ],
        compiler_params=pltpu.CompilerParams(
            collective_id=0, has_side_effects=True, vmem_limit_bytes=56 * 2**20
        ),
    )(
        flat(fields), flat(cotangent), coarse_mask.transpose(2, 0, 1), *consts,
        *[held[name] for name in WEIGHTS],
    )
    shape = (LAT_ROWS, LON_COLS, LEVELS, FINE)
    return tuple(part.reshape(shape).transpose(2, 0, 1, 3) for part in (out, grad))


def solution(mesh):
    placed = (
        P(None, "lat", "lon", None),
        P("lon", None),
        P("lon", None),
        P("lon", None),
        P("lon", None),
        P("lon", None),
        P(None, "lat", "lon"),
        P(None, "lat", "lon", None),
    )

    def body(fields, w_fine_qkv, w_fine_out, w_merge, w_coarse_qkv, w_up, coarse_mask, cotangent):
        weights = (w_fine_qkv, w_fine_out, w_merge, w_up, w_coarse_qkv)
        return run_layer(mesh, fields, cotangent, coarse_mask, weights)

    return jax.shard_map(
        body,
        mesh=mesh,
        in_specs=placed,
        out_specs=(P(None, "lat", "lon", None), P(None, "lat", "lon", None)),
        check_vma=False,
    )
```

```python
import functools
from types import SimpleNamespace

import jax
import jax.numpy as jnp
import ml_dtypes
import numpy as np
from jax import lax
from jax.experimental import pallas as pl
from jax.experimental.pallas import tpu as pltpu
from jax.sharding import PartitionSpec as P

HD = 32
SHLAT = 3
NORM_EPS = 1e-05
FAR_SCORE = -1000000000.0
MASK_PENALTY = 4.0

MESH = pl.DeviceIdType.MESH
OWN = 144
HALO = 48
HALO_REAL = 36
REAL_KEYS = 2 * OWN + 4 * HALO
KEYS = 512
DEPTH = 256
CROWS = 48
CREAL = 36
REAL_CKEYS = 4 * CROWS
CKEYS = 256
FINE = 512
COARSE = 1024
GROUP = 256
HEADS = 8
LEVELS, LAT_ROWS, LON_COLS = 2, 12, 6
LEVEL = LAT_ROWS * LON_COLS


def constants():
    token = np.arange(OWN)
    level, row, col = token // 72, token // 6 % 12, token % 6
    pick = np.zeros((4 * CROWS, OWN), np.float32)
    coarse_at = level * 18 + row // 2 * 3 + col // 2
    pick[(row % 2 * 2 + col % 2) * CROWS + coarse_at, token] = 1
    shrink = pick.reshape(4, CROWS, OWN).sum(0)
    edge = np.zeros((OWN, 4 * HALO), np.float32)
    for slot in range(4):
        low = 9 if slot < 2 else 0
        inside = (row >= low) & (row < low + 3)
        edge[token[inside], slot * HALO + (level * 18 + (row - low) * 6 + col)[inside]] = 1
    bands = np.zeros((8, KEYS), np.float32)
    bands[0] = -1
    own_band = np.where(row < 3, 0, np.where(row < 9, 1, 2))
    bands[0, :OWN] = own_band
    bands[0, OWN : 2 * OWN] = own_band
    for slot in range(4):
        start = 2 * OWN + slot * HALO
        bands[0, start : start + HALO_REAL] = 0 if slot < 2 else 2
        bands[1 + slot // 2, start : start + HALO] = 10
    own_bands = np.zeros((OWN, 128), np.float32) + own_band[:, None]
    rims = np.zeros((2 * HALO, OWN), np.float32)
    for start, low in ((0, 0), (HALO, 9)):
        inside = (row >= low) & (row < low + 3)
        rims[start + (level * 18 + (row - low) * 6 + col)[inside], token[inside]] = 1
    entry = np.arange(CREAL)
    mask_place = np.zeros((18, LEVELS, GROUP), np.float32)
    mask_place[entry % 18, entry // 18, entry] = 1

    def deep(a, depth=DEPTH):
        return np.pad(a, ((0, 0), (0, depth - a.shape[1])))

    return (
        deep(pick), deep(pick.T), deep(shrink), deep(shrink.T, 128), deep(edge),
        deep(rims), bands, own_bands, mask_place,
    )


def mm(a, b):
    return lax.dot_general(a, b, (((1,), (0,)), ((), ())), preferred_element_type=jnp.float32)


def mt(a, b):
    return lax.dot_general(a, b, (((1,), (1,)), ((), ())), preferred_element_type=jnp.float32)


def tm(a, b):
    return lax.dot_general(a, b, (((0,), (0,)), ((), ())), preferred_element_type=jnp.float32)


def short(a):
    return a.astype(jnp.bfloat16)


def wide(a):
    return a.astype(jnp.float32)


def deepened(a, depth=DEPTH):
    return jnp.concatenate([a, jnp.zeros((depth - a.shape[0], a.shape[1]), a.dtype)], axis=0)


def normed_rows(values):
    centre = jnp.mean(values, axis=-1, keepdims=True)
    off = values - centre
    inverse = lax.rsqrt(jnp.mean(off * off, axis=-1, keepdims=True) + NORM_EPS)
    return off * inverse, inverse


def norm_pull(values, grad):
    hat, inverse = normed_rows(values)
    along = jnp.mean(grad * hat, axis=-1, keepdims=True)
    return inverse * (grad - jnp.mean(grad, axis=-1, keepdims=True) - hat * along)


def head_lanes(head):
    return lax.broadcasted_iota(jnp.int32, (1, GROUP), 1) // HD == head


def stack_heads(target, block):
    rows = block.shape[0]
    for head in range(HEADS):
        target[pl.ds(head * rows, rows), :] = jnp.where(
            head_lanes(head), block, jnp.zeros_like(block)
        )


def join_heads(stacked, rows):
    total = jnp.where(head_lanes(0), stacked[:rows], 0.0)
    for head in range(1, HEADS):
        total = total + jnp.where(
            head_lanes(head), stacked[head * rows : (head + 1) * rows], 0.0
        )
    return short(total)


def blocks(count, step):
    def one(index, carry):
        step(index)
        return carry

    lax.fori_loop(0, count, one, 0)


def wide_columns(index, start=0, size=GROUP):
    return pl.ds(pl.multiple_of(start + index * size, size), size)


def lanes(group, start=0):
    if isinstance(group, int):
        return pl.ds(start + group * GROUP, GROUP)
    return pl.ds(pl.multiple_of(start + group * GROUP, GROUP), GROUP)


def attend(rows, channels, q, kv, bias, out, stack, scores, weights, pump):
    together = rows if rows >= OWN else HEADS * rows

    def one_group(group):
        stack_heads(stack, q[:, lanes(group)])
        scores[...] = mt(stack[...], kv[:, lanes(group)])

        def one_head(head, carry):
            spot = pl.ds(pl.multiple_of(head * together, 16), together)
            s = scores[spot, :] * (HD**-0.5) + bias[...]
            e = jnp.exp(s - jnp.max(s, axis=-1, keepdims=True))
            weights[group, spot, :] = short(e * (1.0 / jnp.sum(e, axis=-1, keepdims=True)))
            return carry

        lax.fori_loop(0, HEADS * rows // together, one_head, 0, unroll=8 if together == rows else 1)
        out[:, lanes(group)] = join_heads(mm(weights[group], kv[:, lanes(group, channels)]), rows)
        if pump is not None:
            pump()

    if pump is None:
        blocks(channels // GROUP, one_group)
    else:
        for group in range(channels // GROUP):
            one_group(group)


def attend_pull(rows, channels, q, kv, grad, dq, dkv, stack, scores, weights, inner):
    together = rows if rows >= OWN else HEADS * rows

    def one_group(group, carry):
        stack_heads(stack, grad[:, lanes(group)])
        scores[...] = mt(stack[...], kv[:, lanes(group, channels)])

        def one_head(head, carry):
            spot = pl.ds(pl.multiple_of(head * together, 16), together)
            p = wide(weights[group, spot, :])
            d = scores[spot, :]
            mean = jnp.sum(p * d, axis=-1, keepdims=True)
            inner[spot, :] = short(p * (d - mean) * (HD**-0.5))
            return carry

        lax.fori_loop(0, HEADS * rows // together, one_head, 0, unroll=8 if together == rows else 1)
        dkv[:, lanes(group, channels)] = short(tm(weights[group], stack[...]))
        dq[:, lanes(group)] = join_heads(mm(inner[...], kv[:, lanes(group)]), rows)
        stack_heads(stack, q[:, lanes(group)])
        dkv[:, lanes(group)] = short(tm(inner[...], stack[...]))
        return carry

    lax.fori_loop(0, channels // GROUP, one_group, 0)


def exchange_peers(size_lon, size_lat):
    lon, lat = lax.axis_index("lon"), lax.axis_index("lat")
    odd = lon % 2
    at = lambda lon_at, lat_at: {"lon": lon_at, "lat": lat_at}
    mate = (lon + 2 * odd - 1 + size_lon) % size_lon
    before, after = (lat + size_lat - 1) % size_lat, (lat + 1) % size_lat
    near = lon + 1 - 2 * odd
    step = 2 - 4 * (lon // 2 % 2)
    return SimpleNamespace(
        mate=at(mate, lat),
        before=at(lon, before),
        before_mate=at(mate, before),
        after=at(lon, after),
        after_mate=at(mate, after),
        quad=(at(near, lat), at(lon + step, lat), at(near + step, lat)),
        first=jnp.where(lat == 0, 1.0, 0.0),
        last=jnp.where(lat == size_lat - 1, 1.0, 0.0),
    )


def layer_scratch():
    bf = lambda *s: pltpu.VMEM(s, jnp.bfloat16)
    f32 = lambda *s: pltpu.VMEM(s, jnp.float32)
    return dict(
        xk=bf(KEYS, FINE), masks=f32(4, 8, GROUP),
        kn=bf(4, CROWS, COARSE), dn_send=bf(3, CROWS, COARSE), dn_got=bf(3, CROWS, COARSE),
        df_send=bf(KEYS, FINE), mate_got=bf(OWN, FINE), halo_got=bf(DEPTH, FINE),
        fq=bf(OWN, FINE), fkv=bf(KEYS, 2 * FINE), fbias=f32(OWN, KEYS), mixed=bf(OWN, FINE),
        fstack=bf(HEADS * OWN, GROUP), fscores=f32(HEADS * OWN, KEYS),
        fweights=bf(FINE // GROUP, HEADS * OWN, KEYS), finner=bf(HEADS * OWN, KEYS),
        dmix=bf(OWN, FINE), dfq=bf(OWN, FINE), dfkv=bf(KEYS, 2 * FINE),
        cq=bf(CROWS, COARSE), ckv=bf(CKEYS, 2 * COARSE), cbias=f32(1, CKEYS),
        cmixed=bf(CROWS, COARSE),
        cstack=bf(HEADS * CROWS, GROUP), cscores=f32(HEADS * CROWS, CKEYS),
        cweights=bf(COARSE // GROUP, HEADS * CROWS, CKEYS), cinner=bf(HEADS * CROWS, CKEYS),
        ddeep=bf(CROWS, COARSE), dcq=bf(CROWS, COARSE), dckv=bf(CKEYS, 2 * COARSE),
        skip=bf(OWN, FINE), coarse=bf(CROWS, COARSE), grad_skip=bf(OWN, FINE),
        grouped=bf(CROWS, 4 * FINE), mask_send=f32(4, 8, GROUP), x_in=bf(OWN + 2 * HALO, FINE),
        cot=bf(OWN, FINE),
        w_fq=bf(FINE, 3 * FINE), w_fo=bf(FINE, FINE), xn=bf(KEYS, FINE),
        group_normed=bf(CROWS, 4 * FINE), d_group=f32(CROWS, 4 * FINE),
        d_normed=f32(CROWS, COARSE), d_fine=f32(OWN, FINE), deeper=bf(CROWS, COARSE),
        d_up=bf(CROWS, FINE), d_coarse=bf(CROWS, COARSE), upward=bf(CROWS, FINE),
        fine_mixed=bf(OWN, FINE),
    )


COPIES = 224


def unpack(field, target):
    both = wide(field[...])
    for level in range(LEVELS):
        target[pl.ds(level * LEVEL, LEVEL), :] = short(both[:, level, :])


def pack(values, target):
    halves = [values[level * LEVEL : (level + 1) * LEVEL] for level in range(LEVELS)]
    target[...] = short(jnp.stack(halves, axis=1))


def layer(peers, send, settle, steps, field, cot_field, mask_field, consts, out, grad_out, full, ready, s):
    pick, pick_t, shrink, spread, edge, rims, bands, own_bands, mask_place = consts

    def pump(count=1):
        for _ in range(count):
            next(steps, None)

    def need(name):
        while name not in ready:
            next(steps, None)

    def columns_of(name, index, start=0):
        if name == FQ:
            return s.w_fq[:, wide_columns(index, start)]
        if name == FO:
            return s.w_fo[:, wide_columns(index, start)]
        return full[name][:, :, :, :, wide_columns(index, start)].reshape(-1, GROUP)

    def rows_of(name, index, columns=slice(None)):
        if name in (FQ, FO):
            rows = pl.ds(pl.multiple_of(index * GROUP, GROUP), GROUP)
            return (s.w_fq if name == FQ else s.w_fo)[rows, columns]
        slabs = GROUP // (2 * NY * full[name].shape[3])
        part = full[name][pl.ds(index * slabs, slabs), :, :, :, columns]
        return part.reshape(GROUP, part.shape[-1])

    def project(target, source, name, start=0):
        need(name)

        def step(index):
            target[:, wide_columns(index)] = short(mm(source[...], columns_of(name, index, start)))

        blocks(target.shape[-1] // GROUP, step)

    x_in, cot = s.x_in, s.cot
    unpack(field, x_in)
    rim_rows = mm(short(rims[...]), deepened(x_in[pl.ds(0, OWN), :]))
    x_in[pl.ds(OWN, 2 * HALO), :] = short(rim_rows)
    mask_row = jnp.zeros((1, GROUP), jnp.float32)
    for col in range(3):
        entries = -MASK_PENALTY * (1.0 - mask_field[col].astype(jnp.float32))
        for row in range(6):
            placed = entries[:, row : row + 1] * mask_place[row * 3 + col]
            mask_row = mask_row + jnp.sum(placed, axis=0, keepdims=True)
    lane = lax.broadcasted_iota(jnp.int32, (1, GROUP), 1)
    absent = (lane >= CREAL) & (lane < CROWS)
    mask_row = jnp.broadcast_to(jnp.where(absent, FAR_SCORE, mask_row), (8, GROUP))
    mask_in, masks = s.mask_send, s.masks
    mask_in[0] = mask_row
    for j in range(1, 4):
        mask_in[j] = pltpu.roll(mask_row, j * CROWS, 1)

    xk = s.xk
    top, bottom = x_in.at[pl.ds(OWN, HALO)], x_in.at[pl.ds(OWN + HALO, HALO)]
    slot = lambda ref, i: ref.at[pl.ds(2 * OWN + i * HALO, HALO)]
    opening = [
        send(x_in.at[pl.ds(0, OWN)], xk.at[pl.ds(OWN, OWN)], peers.mate),
        send(bottom, slot(xk, 0), peers.after),
        send(bottom, slot(xk, 1), peers.after_mate),
        send(top, slot(xk, 2), peers.before),
        send(top, slot(xk, 3), peers.before_mate),
    ]
    mask_copies = [
        send(mask_in.at[j + 1], masks.at[j + 1], peers.quad[j]) for j in range(3)
    ]
    pump(2)
    xk[pl.ds(0, OWN), :] = x_in[pl.ds(0, OWN), :]
    xk[pl.ds(REAL_KEYS, KEYS - REAL_KEYS), :] = jnp.zeros((KEYS - REAL_KEYS, FINE), jnp.bfloat16)
    halo_got = s.halo_got
    halo_got[pl.ds(4 * HALO, DEPTH - 4 * HALO), :] = jnp.zeros((DEPTH - 4 * HALO, FINE), jnp.bfloat16)
    masks[0] = mask_in[0]
    key_bands = bands[0:1] + peers.first * bands[1:2] + peers.last * bands[2:3]
    s.fbias[...] = jnp.where(own_bands[:, 0:1] == key_bands, 0.0, FAR_SCORE)
    pump(2)
    unpack(cot_field, cot)
    pump(2)
    for copy in opening:
        copy.wait_recv()

    def norm_step(index):
        rows = pl.ds(pl.multiple_of(index * 128, 128), 128)
        s.xn[rows, :] = short(normed_rows(wide(xk[rows, :]))[0])

    blocks(KEYS // 128, norm_step)
    pump(2)
    project(s.fq, s.xn.at[pl.ds(0, OWN)], FQ)
    project(s.fkv, s.xn, FQ, FINE)
    pump()
    attend(OWN, FINE, s.fq, s.fkv, s.fbias, s.mixed, s.fstack, s.fscores, s.fweights, pump)
    project(s.fine_mixed, s.mixed, FO)
    pump()
    skip = short(wide(x_in[pl.ds(0, OWN), :]) + wide(s.fine_mixed[...]))
    s.skip[...] = skip

    picked = short(mm(short(pick[...]), deepened(skip)))
    for part in range(4):
        s.grouped[:, pl.ds(part * FINE, FINE)] = picked[part * CROWS : (part + 1) * CROWS]
    s.group_normed[...] = short(normed_rows(wide(s.grouped[...]))[0])
    pump()
    project(s.coarse, s.group_normed, MG)
    kn = s.kn
    kn[0] = short(normed_rows(wide(s.coarse[...]))[0])
    quad_copies = [send(kn.at[0], kn.at[j + 1], peers.quad[j]) for j in range(3)]

    cot_here = cot[...]
    s.d_up[...] = short(mm(short(shrink[...]), deepened(cot_here)))
    need(UP)

    def up_step(index):
        s.ddeep[:, wide_columns(index)] = short(mt(s.d_up[...], rows_of(UP, index)))

    blocks(COARSE // GROUP, up_step)
    project(s.cq, kn.at[0], CQ)
    for copy in mask_copies + quad_copies:
        copy.wait_recv()
    total_mask = masks[0] + masks[1] + masks[2] + masks[3]
    s.cbias[...] = jnp.where(lane >= REAL_CKEYS, FAR_SCORE, total_mask[:1, :CKEYS])

    def ckv_step(index):
        s.ckv[pl.ds(0, REAL_CKEYS), wide_columns(index)] = short(
            mm(kn[...].reshape(REAL_CKEYS, COARSE), columns_of(CQ, index, COARSE))
        )

    blocks(2 * COARSE // GROUP, ckv_step)
    s.ckv[pl.ds(REAL_CKEYS, CKEYS - REAL_CKEYS), :] = jnp.zeros(
        (CKEYS - REAL_CKEYS, 2 * COARSE), jnp.bfloat16
    )
    attend(CROWS, COARSE, s.cq, s.ckv, s.cbias, s.cmixed, s.cstack, s.cscores, s.cweights, None)
    s.deeper[...] = short(wide(s.coarse[...]) + wide(s.cmixed[...]))
    project(s.upward, s.deeper, UP)
    output = (wide(s.skip[...]) + mm(short(spread[...]), deepened(s.upward[...], 128)))
    pack(output, out)

    attend_pull(CROWS, COARSE, s.cq, s.ckv, s.ddeep, s.dcq, s.dckv, s.cstack, s.cscores, s.cweights, s.cinner)
    def all_step(index):
        at = wide_columns(index)
        d_all = mt(s.dckv[pl.ds(0, REAL_CKEYS), :], rows_of(CQ, index, pl.ds(COARSE, 2 * COARSE)))
        s.d_normed[:, at] = d_all[:CROWS]
        for j in range(3):
            s.dn_send[j, :, at] = short(d_all[(j + 1) * CROWS : (j + 2) * CROWS])

    blocks(COARSE // GROUP, all_step)
    back_copies = [
        send(s.dn_send.at[j], s.dn_got.at[j], peers.quad[j]) for j in range(3)
    ]

    def own_step(index):
        at = wide_columns(index)
        own_part = mt(s.dcq[...], rows_of(CQ, index, pl.ds(0, COARSE)))
        s.d_normed[:, at] = s.d_normed[:, at] + own_part

    blocks(COARSE // GROUP, own_step)
    settle(len(back_copies))
    for copy in back_copies:
        copy.wait_recv()
    d_normed = s.d_normed[...]
    for j in range(3):
        d_normed = d_normed + wide(s.dn_got[j])
    s.d_coarse[...] = short(wide(s.ddeep[...]) + norm_pull(wide(s.coarse[...]), d_normed))

    def merge_step(index):
        s.d_group[:, wide_columns(index)] = mt(s.d_coarse[...], rows_of(MG, index))

    blocks(4 * FINE // GROUP, merge_step)
    d_group = short(norm_pull(wide(s.grouped[...]), s.d_group[...]))
    d_picked = jnp.concatenate(
        [d_group[:, part * FINE : (part + 1) * FINE] for part in range(4)], axis=0
    )
    s.grad_skip[...] = short(wide(cot_here) + mm(short(pick_t[...]), deepened(d_picked)))

    def out_step(index):
        s.dmix[:, wide_columns(index)] = short(mt(s.grad_skip[...], rows_of(FO, index)))

    blocks(FINE // GROUP, out_step)
    attend_pull(OWN, FINE, s.fq, s.fkv, s.dmix, s.dfq, s.dfkv, s.fstack, s.fscores, s.fweights, s.finner)
    df_send = s.df_send

    def fine_step(index):
        at = wide_columns(index)
        df_all = mt(s.dfkv[...], rows_of(FQ, index, pl.ds(FINE, 2 * FINE)))
        s.d_fine[:, at] = df_all[:OWN]
        df_send[:, at] = short(df_all)

    blocks(FINE // GROUP, fine_step)
    halo_got = s.halo_got
    got = lambda i: halo_got.at[pl.ds(i * HALO, HALO)]
    end_copies = [
        send(df_send.at[pl.ds(OWN, OWN)], s.mate_got, peers.mate),
        send(slot(df_send, 0), got(0), peers.before),
        send(slot(df_send, 1), got(1), peers.before_mate),
        send(slot(df_send, 2), got(2), peers.after),
        send(slot(df_send, 3), got(3), peers.after_mate),
    ]

    def query_step(index):
        at = wide_columns(index)
        own_part = mt(s.dfq[...], rows_of(FQ, index, pl.ds(0, FINE)))
        s.d_fine[:, at] = s.d_fine[:, at] + own_part

    blocks(FINE // GROUP, query_step)
    settle(len(end_copies))
    for copy in end_copies:
        copy.wait_recv()
    d_fine = s.d_fine[...] + wide(s.mate_got[...])
    from_halo = s.fscores.at[pl.ds(0, OWN), :]
    from_halo[...] = mm(short(edge[...]), halo_got[...])
    d_fine = d_fine + from_halo[...]
    pulled = norm_pull(wide(x_in[pl.ds(0, OWN), :]), d_fine)
    pack(wide(s.grad_skip[...]) + pulled, grad_out)


NZ = 8
NY = 4
FQ, FO, MG, UP, CQ = range(5)
WEIGHTS = (FQ, FO, MG, UP, CQ)


def ring_peers():
    lon, lat = lax.axis_index("lon"), lax.axis_index("lat")
    z, y, c = lon // (2 * NY), lon // 2 % NY, lon % 2
    x, y_hi = lat // 2, lat % 2

    def at(dz, dy, core):
        row = y + dy + NY
        carried = (y_hi + row // NY + 1) % 2
        return {
            "lon": ((z + dz + NZ) % NZ * NY + row % NY) * 2 + core,
            "lat": x * 2 + carried,
        }

    peers = at(1, 0, c), at(-1, 0, c), at(0, 1, c), at(0, -1, c), at(0, 0, 1 - c)
    turn = jnp.where(x == 3, 1, -x)
    back = jnp.where(x == 3, -1, x)
    shift_core = jnp.where(x == 0, 1 - c, c)
    shift_to, shift_from = at(0, turn, shift_core), at(0, back, shift_core)
    along = [{"lon": lon, "lat": (x + d) % 4 * 2 + y_hi} for d in (1, 3)]
    rim = tuple(at(d, 0, c) for d in (2, -2, 3, -3, 4))
    return (x, y, z, c), peers + (*along, shift_to, shift_from) + rim


def gather_steps(spot, peers, own, full, send, local_sems, ready, s):
    x, y, z, c = spot
    up_z, down_z, up_y, down_y, twin, up_x, down_x, shift_to, _ = peers[:9]
    w = (x + y) % NY
    z_at = lambda dz: (z + dz + NZ) % NZ
    y_at = lambda dy: (y + dy + NY) % NY
    w_at = lambda dw: (w + dw + NY) % NY
    every = slice(None)
    here = lambda k: full[k].at[z, y, c]

    def arrived(copies):
        for copy in copies:
            copy.wait_recv()

    def pass_on(k, where, peer):
        view = full[k].at[where]
        return send(view, view, peer)

    def half(k, place, which):
        width = full[k].shape[-1] // 2
        return place + (every, pl.ds(which * width, width))

    twins = {name: [] for name in WEIGHTS}

    def to_twin(k, where):
        twins[k].append(pass_on(k, where, twin))

    locals_ = {}
    for index, k in enumerate(WEIGHTS):
        locals_[k] = pltpu.make_async_copy(own[k], here(k), local_sems.at[index])
        if k != CQ:
            locals_[k].start()

    near, far, wheel, ring, across = {}, {}, {}, {}, {}

    def yz_start(k):
        near[k] = [send(own[k], here(k), peer) for peer in (up_y, down_y)]

    def yz_far(k):
        arrived(near[k][:1])
        first = pass_on(k, half(k, (z, y_at(-1), c), 0), up_y)
        arrived(near[k][1:])
        far[k] = [first, pass_on(k, half(k, (z, y_at(1), c), 1), down_y)]

    def yz_round(k):
        arrived(far[k])
        locals_[k].wait()
        wheel[k] = [pass_on(k, (z, every, c), peer) for peer in (up_z, down_z)]
        to_twin(k, (z, every, c))

    def yz_step(k, step):
        arrived(wheel[k])
        if step < 3:
            wheel[k] = [
                pass_on(k, (z_at(-step), every, c), up_z),
                pass_on(k, (z_at(step), every, c), down_z),
            ]
        elif step == 3:
            wheel[k] = [
                pass_on(k, (z_at(-3), pl.ds(0, 2), c), up_z),
                pass_on(k, (z_at(3), pl.ds(2, 2), c), down_z),
            ]
        for d in (-step, step)[: 2 if step < 4 else 1]:
            to_twin(k, (z_at(d), every, c))

    def zy_start(k):
        ring[k] = [send(own[k], here(k), peer) for peer in (up_z, down_z)]

    def zy_step(k, step):
        arrived(ring[k])
        if step < 3:
            ring[k] = [
                pass_on(k, (z_at(-step), y, c), up_z),
                pass_on(k, (z_at(step), y, c), down_z),
            ]
        elif step == 3:
            ring[k] = [
                pass_on(k, half(k, (z_at(-3), y, c), 0), up_z),
                pass_on(k, half(k, (z_at(3), y, c), 1), down_z),
            ]

    def across_y(k, where):
        return [pass_on(k, (where, y, c), peer) for peer in (up_y, down_y)]

    def side(k):
        return (w_at, up_x, down_x) if k == CQ else (y_at, up_y, down_y)

    def chain_across(k, d):
        place, up, down = side(k)
        across[k, d % NZ] = [pass_on(k, (z_at(d), place(0), c), peer) for peer in (up, down)]

    def chain_step(k, step):
        place, _, _ = side(k)
        arrived(ring[k])
        if step < 3:
            ring[k] = [
                pass_on(k, (z_at(-step), place(0), c), up_z),
                pass_on(k, (z_at(step), place(0), c), down_z),
            ]
        elif step == 3:
            ring[k] = [
                pass_on(k, half(k, (z_at(-3), place(0), c), 0), up_z),
                pass_on(k, half(k, (z_at(3), place(0), c), 1), down_z),
            ]
        for d in (-step, step)[: 2 if step < 4 else 1]:
            chain_across(k, d)

    def chain_spread(k, dz, turn):
        place, up, down = side(k)
        arrived(across[k, dz])
        if turn == 0:
            last[k].append(pass_on(k, (z_at(dz), place(-1), c), up))
        else:
            last[k].append(pass_on(k, (z_at(dz), place(1), c), down))

    def chain_twins(k, offsets):
        place, _, _ = side(k)
        for d in offsets:
            to_twin(k, (every, place(d), c))

    last = {CQ: [], MG: []}
    shift = send(own[CQ], here(CQ), shift_to, wait_start=True)

    @pl.when(x == 0)
    def _():
        locals_[CQ].start()

    @pl.when(x > 0)
    def _():
        shift.start()

    fine = (FQ, FO)
    fine_z = [[send(own[k], here(k), peer) for peer in (up_z, down_z) + peers[9:]] for k in fine]
    ring[MG] = [send(own[MG], here(MG), peer) for peer in (up_z, down_z)]

    @pl.when(x == 0)
    def _():
        locals_[CQ].wait()

    @pl.when(x > 0)
    def _():
        shift.wait_recv()

    ring[CQ] = [pass_on(CQ, (z, w, c), peer) for peer in (up_z, down_z)]
    chain_across(CQ, 0)
    yield
    fine_y, fine_far = {}, {}

    def fine_round(k):
        arrived(fine_z[k])
        locals_[k].wait()
        fine_y[k] = across_y(k, every)
        to_twin(k, (every, y, c))

    def fine_spread(k):
        arrived(fine_y[k])
        fine_far[k] = [
            pass_on(k, (pl.ds(0, 4), y_at(-1), c), up_y),
            pass_on(k, (pl.ds(4, 4), y_at(1), c), down_y),
        ]
        to_twin(k, (every, y_at(-1), c))
        to_twin(k, (every, y_at(1), c))

    fine_round(FQ)
    fine_round(FO)
    across[MG, 0] = [send(own[MG], here(MG), peer) for peer in (up_y, down_y)]
    yz_start(UP)
    yield
    chain_step(CQ, 1)
    chain_step(MG, 1)
    yield
    fine_spread(FQ)
    chain_step(CQ, 2)
    chain_step(MG, 2)
    yield
    fine_spread(FO)
    chain_step(CQ, 3)
    chain_step(MG, 3)
    yield
    arrived(fine_far[FQ])
    to_twin(FQ, (every, y_at(2), c))
    chain_step(CQ, 4)
    chain_step(MG, 4)
    arrived(fine_far[FO])
    to_twin(FO, (every, y_at(2), c))
    arrived(twins[FQ])

    def tidy(part):
        columns = wide_columns(part, 0, FINE)
        s.w_fq[:, columns] = short(wide(full[FQ][:, :, :, :, columns]).reshape(FINE, FINE))

    blocks(3, tidy)
    ready.add(FQ)
    yield
    locals_[MG].wait()
    chain_spread(CQ, 0, 0)
    chain_spread(MG, 0, 0)
    chain_twins(CQ, (0,))
    chain_twins(MG, (0,))
    yz_far(UP)
    chain_spread(CQ, 7, 1)
    chain_spread(MG, 7, 1)
    yield
    yz_round(UP)
    arrived(twins[FO])
    s.w_fo[...] = short(wide(full[FO][...]).reshape(FINE, FINE))
    ready.add(FO)
    chain_spread(CQ, 1, 0)
    chain_spread(MG, 1, 0)
    yield
    chain_spread(CQ, 6, 1)
    chain_spread(MG, 6, 1)
    yz_step(UP, 1)
    yield
    chain_spread(CQ, 2, 0)
    chain_spread(MG, 2, 0)
    yield
    chain_spread(CQ, 5, 1)
    chain_spread(MG, 5, 1)
    yz_step(UP, 2)
    yield
    chain_spread(CQ, 3, 0)
    chain_spread(MG, 3, 0)
    yield
    chain_spread(CQ, 4, 1)
    chain_spread(MG, 4, 1)
    chain_twins(MG, (-1, 1))
    chain_twins(CQ, (-1, 1))
    yz_step(UP, 3)
    yield
    arrived(last[MG])
    chain_twins(MG, (2,))
    yield
    arrived(last[CQ])
    chain_twins(CQ, (2,))
    yz_step(UP, 4)
    yield
    arrived(twins[MG])
    ready.add(MG)
    yield
    arrived(twins[CQ])
    ready.add(CQ)
    yield
    arrived(twins[UP])
    ready.add(UP)

    @pl.when(x > 0)
    def _():
        shift.wait_send()


def layer_kernel(size_lon, size_lat, names, *refs):
    field, cot_field, mask_field = refs[:3]
    consts, held = refs[3:12], refs[12:17]
    out, grad_out = refs[17:19]
    scratch = SimpleNamespace(**dict(zip(names, refs[19 : 19 + len(names)])))
    rest = refs[19 + len(names) :]
    full = dict(zip(WEIGHTS, rest[: len(WEIGHTS)]))
    send_sems, recv_sems, local_sems = rest[len(WEIGHTS) :]
    own = dict(zip(WEIGHTS, held))
    peers = exchange_peers(size_lon, size_lat)
    spot, rings = ring_peers()
    barrier = pltpu.get_barrier_semaphore()
    everyone = [peers.mate, peers.before, peers.before_mate, peers.after, peers.after_mate]
    everyone += list(peers.quad) + list(rings)
    for peer in everyone:
        pl.semaphore_signal(barrier, inc=1, device_id=peer, device_id_type=MESH)
    pl.semaphore_wait(barrier, len(everyone))
    started = []

    def send(source, target, peer, wait_start=False):
        index = len(started)
        assert index < COPIES
        copy = pltpu.make_async_remote_copy(
            src_ref=source, dst_ref=target, send_sem=send_sems.at[index],
            recv_sem=recv_sems.at[index], device_id=peer, device_id_type=MESH,
        )
        if not wait_start:
            copy.start()
        started.append(None if wait_start else copy)
        return copy

    settled = [0]

    def settle(but):
        upto = len(started) - but
        for copy in started[settled[0] : upto]:
            if copy is not None:
                copy.wait_send()
        settled[0] = upto

    ready = set()
    steps = gather_steps(spot, rings, own, full, send, local_sems, ready, scratch)
    layer(
        peers, send, settle, steps, field, cot_field, mask_field, consts, out, grad_out, full, ready, scratch
    )
    settle(0)


def run_layer(mesh, fields, cotangent, coarse_mask, held):
    scratch = layer_scratch()
    vmem = pl.BlockSpec(memory_space=pltpu.VMEM)
    rows = (LEVEL, LEVELS, FINE)
    flat = lambda part: part.transpose(1, 2, 0, 3).reshape(rows)
    consts = constants()
    out, grad = pl.pallas_call(
        functools.partial(layer_kernel, mesh.shape["lon"], mesh.shape["lat"], tuple(scratch)),
        out_shape=[jax.ShapeDtypeStruct(rows, jnp.bfloat16)] * 2,
        in_specs=[vmem] * (3 + len(consts)) + [pl.BlockSpec(memory_space=pl.ANY)] * 5,
        out_specs=[vmem] * 2,
        scratch_shapes=list(scratch.values())
        + [pltpu.VMEM((NZ, NY, 2) + held[name].shape, jnp.bfloat16) for name in WEIGHTS]
        + [
            pltpu.SemaphoreType.DMA((COPIES,)),
            pltpu.SemaphoreType.DMA((COPIES,)),
            pltpu.SemaphoreType.DMA((len(WEIGHTS),)),
        ],
        compiler_params=pltpu.CompilerParams(
            collective_id=0, has_side_effects=True, vmem_limit_bytes=56 * 2**20
        ),
    )(
        flat(fields), flat(cotangent), coarse_mask.transpose(2, 0, 1), *consts,
        *[held[name] for name in WEIGHTS],
    )
    shape = (LAT_ROWS, LON_COLS, LEVELS, FINE)
    return tuple(part.reshape(shape).transpose(2, 0, 1, 3) for part in (out, grad))


def solution(mesh):
    placed = (
        P(None, "lat", "lon", None),
        P("lon", None),
        P("lon", None),
        P("lon", None),
        P("lon", None),
        P("lon", None),
        P(None, "lat", "lon"),
        P(None, "lat", "lon", None),
    )

    def body(fields, w_fine_qkv, w_fine_out, w_merge, w_coarse_qkv, w_up, coarse_mask, cotangent):
        weights = (w_fine_qkv, w_fine_out, w_merge, w_up, w_coarse_qkv)
        return run_layer(mesh, fields, cotangent, coarse_mask, weights)

    return jax.shard_map(
        body,
        mesh=mesh,
        in_specs=placed,
        out_specs=(P(None, "lat", "lon", None), P(None, "lat", "lon", None)),
        check_vma=False,
    )
```
